1024 devices in a mesh: dp: 64 (over z, core), owner: 16 (over y, x).
Axes of the slice: x: 4, y: 4, z: 32, core: 2. Of those that a mesh axis runs over, the one named last changes fastest.
Arguments:
- activations: bfloat16 [8192, 4096], P('dp', 'owner'), may hold values from -6 to 6
- weight_tiles: bfloat16 [192, 8, 128, 128], P('owner'), may hold values from -0.1875 to 0.1875
- grad_out: bfloat16 [8192, 24576], P('dp', 'owner'), may hold values from -6 to 6
- tile_rows: int32 [112, 8], replicated, may hold values from 0 to 31, as said below
- col_owner: int32 [112], replicated, may hold values from 0 to 15, as said below
Outputs:
- output: bfloat16 [8192, 24576], P('dp', 'owner')
- grad_input: bfloat16 [8192, 4096], P('dp', 'owner')
- grad_weight: float32 [192, 131072], P('owner', 'dp')
The draws below stay inside these ranges and needn't reach their ends.
Inputs may be any that keep to these rules, and one draw needn't show every extreme that they name: `col_owner`: each owner holds 1 to 12 tile columns and some owner holds exactly 12. The tiles and the output columns of an owner's columns fill its first slots in increasing column order; its other slots are unused. `tile_rows`: each tile column lists 8 distinct tile rows, in no particular order.
All inputs are finite; a program needn't handle non-finite values.
Results may differ from the reference program's by a relative error of at most 0.017.
Values may be sent and summed in bfloat16 or wider, within the bound.
A program may use at most 64 MiB of HBM per device.

```python
import math
import jax
import jax.numpy as jnp
from jax import lax

DIN = 4096
ROWT = 32
COLT = 112
PER_COL = 8
CCAP = 12
TOKENS = 8192
N_OWNER = 16


def draw_tile_rows(key, part):
    scores = jax.random.randint(key, (COLT, ROWT), 0, 1 << 20) * ROWT + jnp.arange(ROWT, dtype=jnp.int32)[None, :]
    ranking = jnp.argsort(scores, axis=1)
    return ranking[:, :PER_COL].astype(jnp.int32)


def draw_col_owner(key, part):
    key_perm, key_pair, key_cols = jax.random.split(key, 3)
    others = N_OWNER - 1
    rest_cols = COLT - CCAP
    base_count = rest_cols // others
    extra_count = rest_cols - base_count * others
    delta_most = max(min(base_count - 1, CCAP - base_count - 1), 0)
    owner_perm = jax.random.permutation(key_perm, N_OWNER).astype(jnp.int32)
    position = jnp.arange(N_OWNER, dtype=jnp.int32)
    counts = jnp.where(position == 0, CCAP, base_count + (position - 1 < extra_count).astype(jnp.int32))
    pair_index = jnp.maximum(position - 1, 0) // 2
    pair_delta = jax.random.randint(key_pair, (N_OWNER,), 0, delta_most + 1)[pair_index]
    first_of_pair = jnp.remainder(jnp.maximum(position - 1, 0), 2) == 0
    count_shift = jnp.where(position == 0, 0, jnp.where(first_of_pair & (position < others), pair_delta, jnp.where(first_of_pair, 0, -pair_delta)))
    counts = (counts + count_shift).astype(jnp.int32)
    bounds = jnp.cumsum(counts).astype(jnp.int32)
    slot_pos = jnp.arange(COLT, dtype=jnp.int32)
    owner_place = jnp.sum((bounds[None, :] <= slot_pos[:, None]).astype(jnp.int32), axis=1)
    slot_owner = owner_perm[owner_place]
    col_perm = jax.random.permutation(key_cols, COLT)
    col_owner = jnp.zeros((COLT,), jnp.int32).at[col_perm].set(slot_owner)
    return col_owner


def levels(key, extent, cuts, low, high):
    def one(dim, parts):
        steps = jax.random.uniform(jax.random.fold_in(jax.random.fold_in(key, 6), dim), (parts,), jnp.float32, low / len(cuts), high / len(cuts))
        return jnp.repeat(jnp.exp(steps), extent[dim] // parts).reshape((-1,) + (1,) * (len(extent) - dim - 1))

    loudness = one(*cuts[0])
    for cut in cuts[1:]:
        loudness = loudness * one(*cut)
    return loudness


def noise(own_key, extent, spread, reach, cuts=(), kind=jnp.bfloat16):
    entries = jax.random.normal(own_key, extent, jnp.float32) * spread
    if len(cuts) > 0:
        entries = levels(own_key, extent, cuts, -0.22, 0.18) * entries
    return jnp.clip(entries, min=-reach, max=reach).astype(kind)


def setup_inputs(seed: int = 0) -> dict:
    streams_of = jax.random.split(jax.random.key(seed), 6)
    activations = noise(streams_of[0], (TOKENS, DIN), 1.0, 6.0, ((0, 64), (1, 16)))
    weight_tiles = noise(streams_of[1], (N_OWNER * CCAP, PER_COL, 128, 128), (PER_COL * 128) ** -0.5, 0.1875, ((0, 16),))
    grad_out = noise(streams_of[2], (TOKENS, N_OWNER * CCAP * 128), 1.0, 6.0, ((0, 64), (1, 16)))
    tile_rows = draw_tile_rows(jax.random.fold_in(streams_of[5], 71), 0)
    col_owner = draw_col_owner(jax.random.fold_in(streams_of[5], 71), 0)
    return dict(activations=activations, weight_tiles=weight_tiles, grad_out=grad_out, tile_rows=tile_rows, col_owner=col_owner)


def slot_lists(col_owner, tile_rows, owner_idx):
    is_mine = (col_owner == owner_idx).astype(jnp.int32)
    col_rank = (jnp.cumsum(is_mine) - 1).astype(jnp.int32)
    slot_ids = jnp.arange(CCAP, dtype=jnp.int32)
    chosen = ((col_rank[None, :] == slot_ids[:, None]) & (is_mine[None, :] == 1)).astype(jnp.int32)
    live_count = lax.optimization_barrier(jnp.sum(chosen, axis=1)).astype(jnp.int32)
    slot_rows = lax.optimization_barrier(jnp.sum(chosen[:, :, None] * tile_rows[None, :, :], axis=1)).astype(jnp.int32)
    return (slot_rows, live_count)

def reference(activations, weight_tiles, grad_out, tile_rows, col_owner):
    tok_count = activations.shape[0]
    input_tiles = activations.reshape(tok_count, ROWT, 128)
    per_owner_w = weight_tiles.reshape(N_OWNER, CCAP, PER_COL, 128, 128)
    per_owner_g = jnp.moveaxis(grad_out.reshape(tok_count, N_OWNER, CCAP, 128), 1, 0)
    grad_scale = 1.0 / math.sqrt(tok_count)
    row_ids = jnp.arange(ROWT, dtype=jnp.int32)

    def visit_owner(running, packed):
        owner_idx, w_own, g_own = packed
        slot_rows, live_count = slot_lists(col_owner, tile_rows, owner_idx)
        live_f = live_count.astype(jnp.float32)[None, :, None]
        picked = input_tiles[:, slot_rows, :].astype(jnp.float32)
        w_f = w_own.astype(jnp.float32)
        product = jnp.einsum('tska,skab->tsb', picked, w_f)
        out_own = (product * live_f).astype(jnp.bfloat16)
        g_live = g_own.astype(jnp.float32) * live_f
        grad_picked = jnp.einsum('tsb,skab->tska', g_live, w_f)
        onehot = (slot_rows.reshape(-1)[:, None] == row_ids[None, :]).astype(jnp.float32)
        owner_term = jnp.einsum('tja,jr->tra', grad_picked.reshape(tok_count, CCAP * PER_COL, 128), onehot, precision=lax.Precision.HIGHEST).reshape(tok_count, DIN)
        rounded = lax.optimization_barrier(owner_term.astype(jnp.bfloat16))
        running = running + rounded.astype(jnp.float32)
        grad_w_own = jnp.einsum('tska,tsb->skab', picked, g_live) * grad_scale
        return (running, (out_own, grad_w_own.reshape(CCAP, PER_COL * 16384)))
    owner_ids = jnp.arange(N_OWNER, dtype=jnp.int32)
    zero_grad = jnp.zeros((tok_count, DIN), jnp.float32)
    grad_total, (out_stack, grad_stack) = lax.scan(visit_owner, zero_grad, (owner_ids, per_owner_w, per_owner_g))
    output = jnp.moveaxis(out_stack, 0, 1).reshape(tok_count, N_OWNER * CCAP * 128)
    return (output, grad_total.astype(jnp.bfloat16), grad_stack.reshape(N_OWNER * CCAP, PER_COL * 16384))
```

```python
import functools
import math

import jax
import jax.numpy as jnp
from jax import lax
from jax.experimental import pallas as pl
from jax.experimental.pallas import tpu as pltpu
from jax.sharding import PartitionSpec as P

MESH = pl.DeviceIdType.MESH
F32 = jnp.float32
BF16 = jnp.bfloat16
PIECES = 3


def kernel(
    dims,
    x_hbm, w_hbm, g_hbm, trt_ref, co_ref,
    out_ref, dx_ref, dw_ref,
    x_ref, xt, sib, xn, w, gcat, gt, dxs, dxr, part, ring_send, ring_recv, tbl, tbl_s,
    in_sem, tbl_sem, gsib_sem, ag_send, ag_recv, sib_send, sib_recv, dx_send, dx_recv, rs_send, rs_recv,
):
    ny, nx, nz, slots, per_col, scale = dims
    owners = ny * nx
    half = nz // 2
    group = slots // PIECES
    row_tiles = 2 * owners
    dp = lax.axis_index("dp")
    me = lax.axis_index("owner")
    z, core = dp // 2, dp % 2
    other = 1 - core
    y, x = me // nx, me % nx

    def dev(d, o):
        return {"dp": d, "owner": o}

    def peer_to(o):
        return ((y + o // nx) % ny) * nx + (x + o % nx) % nx

    def peer_from(o):
        return ((y + ny - o // nx) % ny) * nx + (x + nx - o % nx) % nx

    up = ((z + 1) % nz) * 2 + core
    down = ((z + nz - 1) % nz) * 2 + core
    sibling = z * 2 + other

    x_copy = pltpu.make_async_copy(x_hbm, x_ref, in_sem.at[0])
    g_load = pltpu.make_async_copy(g_hbm, gcat.at[0], in_sem.at[1])
    w_copy = pltpu.make_async_copy(w_hbm, w.at[:, pl.ds(0, per_col)], in_sem.at[2])
    x_copy.start()
    g_load.start()
    w_copy.start()
    g_ref = gcat.at[0]

    barrier = pltpu.get_barrier_semaphore()
    for o in range(1, owners):
        pl.semaphore_signal(barrier, inc=1, device_id=dev(dp, peer_to(o)), device_id_type=MESH)
    for d in (up, down, sibling):
        pl.semaphore_signal(barrier, inc=1, device_id=dev(d, me), device_id_type=MESH)

    x_copy.wait()
    for q in range(2):
        t = x_ref[:, q * 128:(q + 1) * 128].T
        for gi in range(4):
            for h in range(2):
                lo = gi * 32 + h * 16
                xt[2 * me + q, h, gi * 16:(gi + 1) * 16, :] = t[lo:lo + 16, :]
    pl.semaphore_wait(barrier, owners - 1 + 3)

    def ag_copy(o, tile):
        return pltpu.make_async_remote_copy(
            src_ref=xt.at[pl.ds(2 * tile, 2)],
            dst_ref=xt.at[pl.ds(2 * tile, 2)],
            send_sem=ag_send.at[o],
            recv_sem=ag_recv.at[o],
            device_id=dev(dp, peer_to(o)),
            device_id_type=MESH,
        )

    def sib_copy(o, tile):
        return pltpu.make_async_remote_copy(
            src_ref=xt.at[pl.ds(2 * tile, 2), other],
            dst_ref=sib.at[pl.ds(2 * tile, 2)],
            send_sem=sib_send.at[o],
            recv_sem=sib_recv.at[o],
            device_id=dev(sibling, me),
            device_id_type=MESH,
        )

    def dx_copy(o):
        return pltpu.make_async_remote_copy(
            src_ref=dxs.at[o],
            dst_ref=dxr.at[o],
            send_sem=dx_send.at[o],
            recv_sem=dx_recv.at[o],
            device_id=dev(dp, peer_to(o)),
            device_id_type=MESH,
        )

    def ring_copy(way, step, piece):
        return pltpu.make_async_remote_copy(
            src_ref=ring_send.at[way, step, pl.ds(piece * group, group)],
            dst_ref=ring_recv.at[way, step, pl.ds(piece * group, group)],
            send_sem=rs_send.at[way, step, piece],
            recv_sem=rs_recv.at[way, step, piece],
            device_id=dev(up if way == 0 else down, me),
            device_id_type=MESH,
        )

    g_copy = pltpu.make_async_remote_copy(
        src_ref=gcat.at[0],
        dst_ref=gcat.at[1],
        send_sem=gsib_sem.at[0],
        recv_sem=gsib_sem.at[1],
        device_id=dev(sibling, me),
        device_id_type=MESH,
    )

    @pl.loop(1, owners)
    def _(o):
        ag_copy(o, me).start()

    sib_copy(0, me).start()
    g_load.wait()
    g_copy.start()

    n_cols = co_ref.shape[1]
    mine = (co_ref[...] == me).astype(jnp.int32)
    sub = lax.broadcasted_iota(jnp.int32, (n_cols, n_cols), 0)
    lane = lax.broadcasted_iota(jnp.int32, (n_cols, n_cols), 1)
    mine_col = jnp.sum(jnp.where(sub == lane, mine, 0), axis=1, keepdims=True)
    rank = jnp.sum(jnp.where(sub < lane, mine_col, 0), axis=0, keepdims=True)
    slot_id = lax.broadcasted_iota(jnp.int32, (16, n_cols), 0)
    chosen = jnp.where((rank == slot_id) & (slot_id < slots), mine, 0)
    live_col = jnp.sum(chosen, axis=1, keepdims=True)
    tl = lax.broadcasted_iota(jnp.int32, (16, 128), 1)
    table = jnp.where(tl < row_tiles, per_col, 0)
    for k in range(per_col):
        row_col = jnp.sum(chosen * trt_ref[k:k + 1, :], axis=1, keepdims=True)
        found = (live_col == 1) & (tl < row_tiles) & (tl == row_col)
        table = jnp.where(found, k, jnp.where(tl == row_tiles + k, row_col, table))
    table = jnp.where(tl == row_tiles + per_col, live_col, table)
    tbl[...] = table
    tbl_copy = pltpu.make_async_copy(tbl, tbl_s, tbl_sem)
    tbl_copy.start()

    for s in range(slots):
        w[s, per_col] = jnp.zeros((128, 128), BF16)
        gt[s * 128:(s + 1) * 128, :] = g_ref[:, s * 128:(s + 1) * 128].T

    tbl_copy.wait()
    w_copy.wait()

    def dx_terms(o):
        owner = peer_to(o)
        for q in range(2):
            r = 2 * owner + q
            lhs = jnp.concatenate([w[s, tbl_s[s, r]] for s in range(slots)], axis=1)
            dxs[o, q] = jnp.dot(lhs, gt[...], preferred_element_type=F32).astype(BF16)

    @pl.loop(1, owners)
    def _(o):
        dx_terms(o)
        ag_copy(o, peer_from(o)).wait_recv()
        sib_copy(o, peer_from(o)).start()

    @pl.loop(1, owners)
    def _(o):
        dx_copy(o).start()

    @pl.loop(0, owners)
    def _(o):
        sib_copy(o, peer_from(o)).wait_recv()

    g_copy.wait_recv()

    def dw_terms(s):
        rows = [tbl_s[s, row_tiles + k] for k in range(per_col)]
        lhs = jnp.concatenate(
            [jnp.concatenate([xt[rk, core] for rk in rows], axis=0), jnp.concatenate([sib[rk] for rk in rows], axis=0)],
            axis=1,
        )
        lanes = pl.ds(pl.multiple_of(s * 128, 128), 128)
        rhs = jnp.concatenate([gcat[0, :, lanes], gcat[1, :, lanes]], axis=0)
        res = jnp.dot(lhs, rhs, preferred_element_type=F32)
        for c in range(4 * per_col):
            part[c, s] = res[c * 16:(c + 1) * 16, :]

    def dest(way, step):
        return (z + half - step) % nz if way == 0 else (z + nz - (half - 1 - step)) % nz

    def send_sum(way, step, piece, first):
        at = pl.ds(piece * group, group)
        total = part[dest(way, step), at]
        if not first:
            ring_copy(way, step - 1, piece).wait_recv()
            total = total + ring_recv[way, step - 1, at].astype(F32)
        ring_send[way, step, at] = total.astype(BF16)
        ring_copy(way, step, piece).start()

    for piece in range(PIECES):
        @pl.loop(piece * group, (piece + 1) * group)
        def _(s):
            dw_terms(s)
        for way in range(2):
            send_sum(way, 0, piece, True)

    turn_steps = 4
    turn_tiles = row_tiles // turn_steps

    def unit(u):
        @pl.when(u < turn_steps)
        def _():
            for j in range(turn_tiles):
                r = u * turn_tiles + j
                t = jnp.concatenate([xt[r, h, gi * 16:(gi + 1) * 16, :] for gi in range(4) for h in range(2)], axis=0)
                xn[r] = t.T

        @pl.when((u >= turn_steps) & (u < turn_steps + slots))
        def _():
            s = u - turn_steps
            lhs = jnp.concatenate([xn[tbl_s[s, row_tiles + k]] for k in range(per_col)], axis=1)
            rhs = jnp.concatenate([w[s, k] for k in range(per_col)], axis=0)
            live = tbl_s[s, row_tiles + per_col].astype(F32)
            out = jnp.dot(lhs, rhs, preferred_element_type=F32) * live
            out_ref[:, pl.ds(pl.multiple_of(s * 128, 128), 128)] = out.astype(BF16)

    @pl.loop(1, half - 1)
    def _(step):
        for piece in range(PIECES):
            for way in range(2):
                send_sum(way, step, piece, False)
        unit(step - 1)

    for piece in range(PIECES):
        send_sum(0, half - 1, piece, False)

    @pl.loop(half - 2, turn_steps + slots)
    def _(u):
        unit(u)

    dx_terms(0)

    def dx_add(o, total):
        dx_copy(o).wait_recv()
        return total + dxr[o].astype(F32)

    dx = lax.fori_loop(1, owners, dx_add, dxs[0].astype(F32))
    for q in range(2):
        dx_ref[:, q * 128:(q + 1) * 128] = dx[q].T.astype(BF16)

    for piece in range(PIECES):
        at = pl.ds(piece * group, group)
        ring_copy(1, half - 2, piece).wait_recv()
        total = part[z, at] + ring_recv[1, half - 2, at].astype(F32)
        ring_copy(0, half - 1, piece).wait_recv()
        total = total + ring_recv[0, half - 1, at].astype(F32)
        for i in range(group):
            s = piece * group + i
            live = tbl_s[s, row_tiles + per_col].astype(F32)
            dw_ref[s] = total[i] * (live * scale)

    @pl.loop(1, owners)
    def _(o):
        ag_copy(o, me).wait_send()
        dx_copy(o).wait_send()

    @pl.loop(0, owners)
    def _(o):
        sib_copy(o, me).wait_send()

    g_copy.wait_send()

    @pl.loop(0, half - 1)
    def _(step):
        for piece in range(PIECES):
            for way in range(2):
                ring_copy(way, step, piece).wait_send()

    for piece in range(PIECES):
        ring_copy(0, half - 1, piece).wait_send()


def local(ny, nx, n_dp, activations, weight_tiles, grad_out, tile_rows, col_owner):
    tokens, features = activations.shape
    slots, per_col = weight_tiles.shape[:2]
    owners = ny * nx
    nz = n_dp // 2
    half = nz // 2
    row_tiles = 2 * owners
    scale = 1.0 / math.sqrt(tokens * n_dp)
    vmem = pl.BlockSpec(memory_space=pltpu.VMEM)
    hbm = pl.BlockSpec(memory_space=pltpu.HBM)
    dma = pltpu.SemaphoreType.DMA
    out, dx, dw = pl.pallas_call(
        functools.partial(kernel, (ny, nx, nz, slots, per_col, scale)),
        out_shape=(
            jax.ShapeDtypeStruct(grad_out.shape, BF16),
            jax.ShapeDtypeStruct(activations.shape, BF16),
            jax.ShapeDtypeStruct((slots, 16, 128), F32),
        ),
        in_specs=[hbm, hbm, hbm, vmem, vmem],
        out_specs=(vmem, vmem, vmem),
        scratch_shapes=[
            pltpu.VMEM(activations.shape, BF16),
            pltpu.VMEM((row_tiles, 2, 64, tokens), BF16),
            pltpu.VMEM((row_tiles, 64, tokens), BF16),
            pltpu.VMEM((row_tiles, tokens, 128), BF16),
            pltpu.VMEM((slots, per_col + 1, 128, 128), BF16),
            pltpu.VMEM((2, tokens, slots * 128), BF16),
            pltpu.VMEM((slots * 128, tokens), BF16),
            pltpu.VMEM((owners, 2, 128, tokens), BF16),
            pltpu.VMEM((owners, 2, 128, tokens), BF16),
            pltpu.VMEM((nz, slots, 16, 128), F32),
            pltpu.VMEM((2, half, slots, 16, 128), BF16),
            pltpu.VMEM((2, half, slots, 16, 128), BF16),
            pltpu.VMEM((16, 128), jnp.int32),
            pltpu.SMEM((16, 128), jnp.int32),
            dma((3,)),
            dma(()),
            dma((2,)),
            dma((owners,)),
            dma((owners,)),
            dma((owners,)),
            dma((owners,)),
            dma((owners,)),
            dma((owners,)),
            dma((2, half, PIECES)),
            dma((2, half, PIECES)),
        ],
        compiler_params=pltpu.CompilerParams(
            collective_id=0, has_side_effects=True, vmem_limit_bytes=60 * 1024 * 1024
        ),
    )(activations, weight_tiles, grad_out, tile_rows.T, col_owner.reshape(1, -1))
    return out, dx, dw.reshape(slots, 2048)


def solution(mesh):
    owners, n_dp = mesh.shape["owner"], mesh.shape["dp"]
    nx = math.isqrt(owners)
    in_specs = (P("dp", "owner"), P("owner", None, None, None), P("dp", "owner"), P(), P())
    out_specs = (P("dp", "owner"), P("dp", "owner"), P("owner", "dp"))
    return jax.shard_map(
        functools.partial(local, owners // nx, nx, n_dp),
        mesh=mesh,
        in_specs=in_specs,
        out_specs=out_specs,
        check_vma=False,
    )
```

```python
import functools
import math

import jax
import jax.numpy as jnp
from jax import lax
from jax.experimental import pallas as pl
from jax.experimental.pallas import tpu as pltpu
from jax.sharding import PartitionSpec as P

MESH = pl.DeviceIdType.MESH
F32 = jnp.float32
BF16 = jnp.bfloat16
PIECES = 3
NEAR = [(1, 1), (1, -1), (-1, 1), (-1, -1), (0, 1), (0, -1), (1, 0), (-1, 0)]
FAR = [(0, 2), (1, 2), (-1, 2), (2, 0), (2, 1), (2, -1), (2, 2)]


def kernel(
    dims,
    x_hbm, w_hbm, g_hbm, trt_ref, co_ref,
    out_ref, dx_ref, dw_ref,
    x_ref, xt, sib, xn, w, gcat, gt, dxs, dxr, part, pair_send, pair_recv, chain_send, chain_recv, tbl, tbl_s,
    in_sem, tbl_sem, gsib_sem, ag_send, ag_recv, rl_send, rl_recv, sib_send, sib_recv, dx_send, dx_recv,
    ps_send, ps_recv, cs_send, cs_recv,
):
    ny, nx, nz, slots, per_col, scale = dims
    owners = ny * nx
    half = nz // 2
    steps = half // 2
    group = slots // PIECES
    row_tiles = 2 * owners
    dp = lax.axis_index("dp")
    me = lax.axis_index("owner")
    z, core = dp // 2, dp % 2
    other = 1 - core
    y, x = me // nx, me % nx

    def dev(d, o):
        return {"dp": d, "owner": o}

    def peer_to(o):
        return ((y + o // nx) % ny) * nx + (x + o % nx) % nx

    def shift(v):
        return ((y + ny + v[0]) % ny) * nx + (x + nx + v[1]) % nx

    def along(way, links):
        return dev(((z + links) % nz if way == 0 else (z + nz - links) % nz) * 2 + core, me)

    sibling = z * 2 + other

    x_copy = pltpu.make_async_copy(x_hbm, x_ref, in_sem.at[0])
    g_load = pltpu.make_async_copy(g_hbm, gcat.at[0], in_sem.at[1])
    w_copy = pltpu.make_async_copy(w_hbm, w.at[:, pl.ds(0, per_col)], in_sem.at[2])
    x_copy.start()
    g_load.start()
    w_copy.start()
    g_ref = gcat.at[0]

    barrier = pltpu.get_barrier_semaphore()
    for o in range(1, owners):
        pl.semaphore_signal(barrier, inc=1, device_id=dev(dp, peer_to(o)), device_id_type=MESH)
    for d in (along(0, 1), along(1, 1), along(0, 2), along(1, 2), dev(sibling, me)):
        pl.semaphore_signal(barrier, inc=1, device_id=d, device_id_type=MESH)

    x_copy.wait()
    for q in range(2):
        t = x_ref[:, q * 128:(q + 1) * 128].T
        for gi in range(4):
            for h in range(2):
                lo = gi * 32 + h * 16
                xt[2 * me + q, h, gi * 16:(gi + 1) * 16, :] = t[lo:lo + 16, :]
    pl.semaphore_wait(barrier, owners - 1 + 5)

    def plane_copy(tile, at, n, send, recv, move):
        here = pl.ds(2 * tile + at, n)
        return pltpu.make_async_remote_copy(
            src_ref=xt.at[here],
            dst_ref=xt.at[here],
            send_sem=send,
            recv_sem=recv,
            device_id=dev(dp, shift(move)),
            device_id_type=MESH,
        )

    def quarter_copy(tile, q, h, send, recv, move):
        return pltpu.make_async_remote_copy(
            src_ref=xt.at[2 * tile + q, h],
            dst_ref=xt.at[2 * tile + q, h],
            send_sem=send,
            recv_sem=recv,
            device_id=dev(dp, shift(move)),
            device_id_type=MESH,
        )

    def near_copy(v, tile):
        i = NEAR.index(v)
        return plane_copy(tile, 0, 2, ag_send.at[i], ag_recv.at[i], v)

    def relay_copies(v, tile):
        dy, dx = v
        i = NEAR.index(v)
        out = []
        if dx:
            q = 0 if dx > 0 else 1
            out.append(plane_copy(tile, q, 1, rl_send.at[0, i], rl_recv.at[0, i], (0, dx)))
        if dy:
            q = 0 if dy > 0 else 1
            out.append(plane_copy(tile, q, 1, rl_send.at[1, i], rl_recv.at[1, i], (dy, 0)))
        if dx and dy:
            q, h = 0 if dy > 0 else 1, 0 if dx > 0 else 1
            out.append(quarter_copy(tile, q, h, rl_send.at[2, i], rl_recv.at[2, i], v))
        return out

    def relayed_copies(u, tile):
        dy, dx = u
        out = []
        if dx == 2 and dy != 2:
            for d in (1, -1):
                out.append(relay_copies((dy, d), tile)[0])
        elif dy == 2 and dx != 2:
            for d in (1, -1):
                out.append(relay_copies((d, dx), tile)[1 if dx else 0])
        else:
            for d in (1, -1):
                for e in (1, -1):
                    out.append(relay_copies((d, e), tile)[2])
        return out

    def sib_copy(i, tile):
        return pltpu.make_async_remote_copy(
            src_ref=xt.at[pl.ds(2 * tile, 2), other],
            dst_ref=sib.at[pl.ds(2 * tile, 2)],
            send_sem=sib_send.at[i],
            recv_sem=sib_recv.at[i],
            device_id=dev(sibling, me),
            device_id_type=MESH,
        )

    def dx_copy(o):
        return pltpu.make_async_remote_copy(
            src_ref=dxs.at[o],
            dst_ref=dxr.at[o],
            send_sem=dx_send.at[o],
            recv_sem=dx_recv.at[o],
            device_id=dev(dp, peer_to(o)),
            device_id_type=MESH,
        )

    def pair_copy(way, step, piece):
        at = pl.ds(piece * group, group)
        return pltpu.make_async_remote_copy(
            src_ref=pair_send.at[way, step, at],
            dst_ref=pair_recv.at[way, step, at],
            send_sem=ps_send.at[way, step, piece],
            recv_sem=ps_recv.at[way, step, piece],
            device_id=along(way, 1),
            device_id_type=MESH,
        )

    def chain_copy(way, step, piece, links=2):
        at = pl.ds(piece * group, group)
        return pltpu.make_async_remote_copy(
            src_ref=chain_send.at[way, step, at],
            dst_ref=chain_recv.at[way, step, at],
            send_sem=cs_send.at[way, step, piece],
            recv_sem=cs_recv.at[way, step, piece],
            device_id=along(way, links),
            device_id_type=MESH,
        )

    g_copy = pltpu.make_async_remote_copy(
        src_ref=gcat.at[0],
        dst_ref=gcat.at[1],
        send_sem=gsib_sem.at[0],
        recv_sem=gsib_sem.at[1],
        device_id=dev(sibling, me),
        device_id_type=MESH,
    )

    for v in NEAR:
        near_copy(v, me).start()

    sib_copy(0, me).start()
    g_load.wait()
    g_copy.start()

    n_cols = co_ref.shape[1]
    mine = (co_ref[...] == me).astype(jnp.int32)
    sub = lax.broadcasted_iota(jnp.int32, (n_cols, n_cols), 0)
    lane = lax.broadcasted_iota(jnp.int32, (n_cols, n_cols), 1)
    mine_col = jnp.sum(jnp.where(sub == lane, mine, 0), axis=1, keepdims=True)
    rank = jnp.sum(jnp.where(sub < lane, mine_col, 0), axis=0, keepdims=True)
    slot_id = lax.broadcasted_iota(jnp.int32, (16, n_cols), 0)
    chosen = jnp.where((rank == slot_id) & (slot_id < slots), mine, 0)
    live_col = jnp.sum(chosen, axis=1, keepdims=True)
    tl = lax.broadcasted_iota(jnp.int32, (16, 128), 1)
    table = jnp.where(tl < row_tiles, per_col, 0)
    for k in range(per_col):
        row_col = jnp.sum(chosen * trt_ref[k:k + 1, :], axis=1, keepdims=True)
        found = (live_col == 1) & (tl < row_tiles) & (tl == row_col)
        table = jnp.where(found, k, jnp.where(tl == row_tiles + k, row_col, table))
    table = jnp.where(tl == row_tiles + per_col, live_col, table)
    tbl[...] = table
    tbl_copy = pltpu.make_async_copy(tbl, tbl_s, tbl_sem)
    tbl_copy.start()

    for s in range(slots):
        w[s, per_col] = jnp.zeros((128, 128), BF16)
        gt[s * 128:(s + 1) * 128, :] = g_ref[:, s * 128:(s + 1) * 128].T

    tbl_copy.wait()
    w_copy.wait()

    def dx_terms(o):
        owner = peer_to(o)
        for q in range(2):
            r = 2 * owner + q
            lhs = jnp.concatenate([w[s, tbl_s[s, r]] for s in range(slots)], axis=1)
            dxs[o, q] = jnp.dot(lhs, gt[...], preferred_element_type=F32).astype(BF16)

    early = 1 + (owners - 1) * 2 // 5

    @pl.loop(1, early)
    def _(o):
        dx_terms(o)

    for i, v in enumerate(NEAR):
        tile = shift((-v[0], -v[1]))
        near_copy(v, tile).wait_recv()
        for copy in relay_copies(v, tile):
            copy.start()
        sib_copy(1 + i, tile).start()

    @pl.loop(early, owners)
    def _(o):
        dx_terms(o)

    for i, u in enumerate(FAR):
        tile = shift((-u[0], -u[1]))
        for copy in relayed_copies(u, tile):
            copy.wait_recv()
        sib_copy(1 + len(NEAR) + i, tile).start()

    @pl.loop(1, owners)
    def _(o):
        dx_copy(o).start()

    sib_copy(0, me).wait_recv()
    for i, v in enumerate(NEAR + FAR):
        sib_copy(1 + i, shift((-v[0], -v[1]))).wait_recv()

    g_copy.wait_recv()

    def dw_terms(s):
        rows = [tbl_s[s, row_tiles + k] for k in range(per_col)]
        lhs = jnp.concatenate(
            [jnp.concatenate([xt[rk, core] for rk in rows], axis=0), jnp.concatenate([sib[rk] for rk in rows], axis=0)],
            axis=1,
        )
        lanes = pl.ds(pl.multiple_of(s * 128, 128), 128)
        rhs = jnp.concatenate([gcat[0, :, lanes], gcat[1, :, lanes]], axis=0)
        res = jnp.dot(lhs, rhs, preferred_element_type=F32)
        for c in range(4 * per_col):
            part[c, s] = res[c * 16:(c + 1) * 16, :]

    def dest(way, links):
        return (z + links) % nz if way == 0 else (z + nz - links) % nz

    def send_pair(way, step, piece):
        at = pl.ds(piece * group, group)
        pair_send[way, step, at] = part[dest(way, half - 2 * step), at].astype(BF16)
        pair_copy(way, step, piece).start()

    def send_chain(way, step, piece, paired=True, chained=True, links=2):
        at = pl.ds(piece * group, group)
        total = part[dest(way, half - 1 - 2 * step), at]
        if paired:
            pair_copy(way, step, piece).wait_recv()
            total = total + pair_recv[way, step, at].astype(F32)
        if chained:
            chain_copy(way, step - 1, piece).wait_recv()
            total = total + chain_recv[way, step - 1, at].astype(F32)
        chain_send[way, step, at] = total.astype(BF16)
        chain_copy(way, step, piece, links).start()

    for piece in range(PIECES):
        @pl.loop(piece * group, (piece + 1) * group)
        def _(s):
            dw_terms(s)
        send_pair(0, 0, piece)
        send_chain(1, 0, piece, paired=False, chained=False, links=2 if steps > 1 else 1)

    turn_steps = 4
    turn_tiles = row_tiles // turn_steps

    def unit(u):
        @pl.when(u < turn_steps)
        def _():
            for j in range(turn_tiles):
                r = u * turn_tiles + j
                t = jnp.concatenate([xt[r, h, gi * 16:(gi + 1) * 16, :] for gi in range(4) for h in range(2)], axis=0)
                xn[r] = t.T

        @pl.when((u >= turn_steps) & (u < turn_steps + slots))
        def _():
            s = u - turn_steps
            lhs = jnp.concatenate([xn[tbl_s[s, row_tiles + k]] for k in range(per_col)], axis=1)
            rhs = jnp.concatenate([w[s, k] for k in range(per_col)], axis=0)
            live = tbl_s[s, row_tiles + per_col].astype(F32)
            out = jnp.dot(lhs, rhs, preferred_element_type=F32) * live
            out_ref[:, pl.ds(pl.multiple_of(s * 128, 128), 128)] = out.astype(BF16)

    per_step = (turn_steps + slots) // steps

    def units(step):
        for u in range(per_step):
            unit(step * per_step + u)

    for piece in range(PIECES):
        send_chain(0, 0, piece, chained=False, links=2 if steps > 1 else 1)
        if steps > 1:
            send_pair(0, 1, piece)
            send_pair(1, 1, piece)
    units(0)

    @pl.loop(1, steps - 1)
    def _(step):
        for piece in range(PIECES):
            for way in range(2):
                send_chain(way, step, piece)
            for way in range(2):
                send_pair(way, step + 1, piece)
        units(step)

    if steps > 1:
        for piece in range(PIECES):
            for way in range(2):
                send_chain(way, steps - 1, piece, links=1)
        units(steps - 1)

    dx_terms(0)

    def dx_add(o, total):
        dx_copy(o).wait_recv()
        return total + dxr[o].astype(F32)

    dx = lax.fori_loop(1, owners, dx_add, dxs[0].astype(F32))
    for q in range(2):
        dx_ref[:, q * 128:(q + 1) * 128] = dx[q].T.astype(BF16)

    totals = []
    for piece in range(PIECES):
        at = pl.ds(piece * group, group)
        total = part[z, at]
        for way in range(2):
            chain_copy(way, steps - 1, piece).wait_recv()
            total = total + chain_recv[way, steps - 1, at].astype(F32)
        totals += [total[i] * (tbl_s[piece * group + i, row_tiles + per_col].astype(F32) * scale) for i in range(group)]
    total = jnp.stack(totals)
    for i in range(16):
        dw_ref[:, i * 128:(i + 1) * 128] = total[:, i, :]

    @pl.loop(1, owners)
    def _(o):
        dx_copy(o).wait_send()

    for v in NEAR:
        near_copy(v, me).wait_send()
        for copy in relay_copies(v, me):
            copy.wait_send()

    @pl.loop(0, owners)
    def _(i):
        sib_copy(i, me).wait_send()

    g_copy.wait_send()

    for way in range(2):
        for piece in range(PIECES):
            chain_copy(way, 0, piece).wait_send()
            if way == 0:
                pair_copy(way, 0, piece).wait_send()

    @pl.loop(1, steps)
    def _(step):
        for piece in range(PIECES):
            for way in range(2):
                chain_copy(way, step, piece).wait_send()
                pair_copy(way, step, piece).wait_send()


def finish(a_ref, b_ref, c_ref, x_ref, y_ref, z_ref, a, b, c, load_sem, store_sem):
    loads, stores = [], []
    for i, (src, held, dst) in enumerate(((a_ref, a, x_ref), (b_ref, b, y_ref), (c_ref, c, z_ref))):
        loads.append(pltpu.make_async_copy(src, held, load_sem.at[i]))
        stores.append(pltpu.make_async_copy(held, dst, store_sem.at[i]))
    for load in loads:
        load.start()
    for load, store in zip(loads, stores):
        load.wait()
        store.start()
    for store in stores:
        store.wait()


def local(ny, nx, n_dp, activations, weight_tiles, grad_out, tile_rows, col_owner):
    tokens, features = activations.shape
    slots, per_col = weight_tiles.shape[:2]
    owners = ny * nx
    nz = n_dp // 2
    steps = nz // 4
    row_tiles = 2 * owners
    scale = 1.0 / math.sqrt(tokens * n_dp)
    vmem = pl.BlockSpec(memory_space=pltpu.VMEM)
    hbm = pl.BlockSpec(memory_space=pltpu.HBM)
    dma = pltpu.SemaphoreType.DMA
    results = pl.pallas_call(
        functools.partial(kernel, (ny, nx, nz, slots, per_col, scale)),
        out_shape=(
            jax.ShapeDtypeStruct(grad_out.shape, BF16),
            jax.ShapeDtypeStruct(activations.shape, BF16),
            jax.ShapeDtypeStruct((slots, 2048), F32),
        ),
        in_specs=[hbm, hbm, hbm, vmem, vmem],
        out_specs=(vmem, vmem, vmem),
        scratch_shapes=[
            pltpu.VMEM(activations.shape, BF16),
            pltpu.VMEM((row_tiles, 2, 64, tokens), BF16),
            pltpu.VMEM((row_tiles, 64, tokens), BF16),
            pltpu.VMEM((row_tiles, tokens, 128), BF16),
            pltpu.VMEM((slots, per_col + 1, 128, 128), BF16),
            pltpu.VMEM((2, tokens, slots * 128), BF16),
            pltpu.VMEM((slots * 128, tokens), BF16),
            pltpu.VMEM((owners, 2, 128, tokens), BF16),
            pltpu.VMEM((owners, 2, 128, tokens), BF16),
            pltpu.VMEM((nz, slots, 16, 128), F32),
            pltpu.VMEM((2, steps, slots, 16, 128), BF16),
            pltpu.VMEM((2, steps, slots, 16, 128), BF16),
            pltpu.VMEM((2, steps, slots, 16, 128), BF16),
            pltpu.VMEM((2, steps, slots, 16, 128), BF16),
            pltpu.VMEM((16, 128), jnp.int32),
            pltpu.SMEM((16, 128), jnp.int32),
            dma((3,)),
            dma(()),
            dma((2,)),
            dma((8,)),
            dma((8,)),
            dma((3, 8)),
            dma((3, 8)),
            dma((owners,)),
            dma((owners,)),
            dma((owners,)),
            dma((owners,)),
            dma((2, steps, PIECES)),
            dma((2, steps, PIECES)),
            dma((2, steps, PIECES)),
            dma((2, steps, PIECES)),
        ],
        compiler_params=pltpu.CompilerParams(
            collective_id=0, has_side_effects=True, vmem_limit_bytes=60 * 1024 * 1024
        ),
    )(activations, weight_tiles, grad_out, tile_rows.T, col_owner.reshape(1, -1))
    return pl.pallas_call(
        finish,
        out_shape=tuple(jax.ShapeDtypeStruct(r.shape, r.dtype) for r in results),
        in_specs=[hbm] * 3,
        out_specs=(hbm,) * 3,
        scratch_shapes=[pltpu.VMEM(r.shape, r.dtype) for r in results] + [dma((3,)), dma((3,))],
    )(*results)


def solution(mesh):
    owners, n_dp = mesh.shape["owner"], mesh.shape["dp"]
    nx = math.isqrt(owners)
    in_specs = (P("dp", "owner"), P("owner", None, None, None), P("dp", "owner"), P(), P())
    out_specs = (P("dp", "owner"), P("dp", "owner"), P("owner", "dp"))
    return jax.shard_map(
        functools.partial(local, owners // nx, nx, n_dp),
        mesh=mesh,
        in_specs=in_specs,
        out_specs=out_specs,
        check_vma=False,
    )
```

```python
import functools
import math

import jax
import jax.numpy as jnp
from jax import lax
from jax.experimental import pallas as pl
from jax.experimental.pallas import tpu as pltpu
from jax.sharding import PartitionSpec as P

MESH = pl.DeviceIdType.MESH
F32 = jnp.float32
BF16 = jnp.bfloat16
PIECES = 3
NEAR = [(1, 1), (1, -1), (-1, 1), (-1, -1), (0, 1), (0, -1), (1, 0), (-1, 0)]
FAR = [(0, 2), (1, 2), (-1, 2), (2, 0), (2, 1), (2, -1), (2, 2)]


def kernel(
    dims,
    x_hbm, w_hbm, g_hbm, trt_ref, co_ref,
    out_ref, dx_ref, dw_ref,
    x_ref, xt, sib, xn, w, gcat, gt, dxs, dxr, part, pair_send, pair_recv, chain_send, chain_recv, tbl, tbl_s,
    in_sem, tbl_sem, gsib_sem, ag_send, ag_recv, rl_send, rl_recv, sib_send, sib_recv, dx_send, dx_recv,
    ps_send, ps_recv, cs_send, cs_recv,
):
    ny, nx, nz, slots, per_col, scale = dims
    owners = ny * nx
    half = nz // 2
    steps = half // 2
    group = slots // PIECES
    row_tiles = 2 * owners
    dp = lax.axis_index("dp")
    me = lax.axis_index("owner")
    z, core = dp // 2, dp % 2
    other = 1 - core
    y, x = me // nx, me % nx

    def dev(d, o):
        return {"dp": d, "owner": o}

    def peer_to(o):
        return ((y + o // nx) % ny) * nx + (x + o % nx) % nx

    def shift(v):
        return ((y + ny + v[0]) % ny) * nx + (x + nx + v[1]) % nx

    def along(way, links):
        return dev(((z + links) % nz if way == 0 else (z + nz - links) % nz) * 2 + core, me)

    sibling = z * 2 + other

    x_copy = pltpu.make_async_copy(x_hbm, x_ref, in_sem.at[0])
    g_load = pltpu.make_async_copy(g_hbm, gcat.at[0], in_sem.at[1])
    w_copy = pltpu.make_async_copy(w_hbm, w.at[:, pl.ds(0, per_col)], in_sem.at[2])
    x_copy.start()
    g_load.start()
    w_copy.start()
    g_ref = gcat.at[0]

    barrier = pltpu.get_barrier_semaphore()
    for o in range(1, owners):
        pl.semaphore_signal(barrier, inc=1, device_id=dev(dp, peer_to(o)), device_id_type=MESH)
    for d in (along(0, 1), along(1, 1), along(0, 2), along(1, 2), dev(sibling, me)):
        pl.semaphore_signal(barrier, inc=1, device_id=d, device_id_type=MESH)

    x_copy.wait()
    for q in range(2):
        t = x_ref[:, q * 128:(q + 1) * 128].T
        for gi in range(4):
            for h in range(2):
                lo = gi * 32 + h * 16
                xt[2 * me + q, h, gi * 16:(gi + 1) * 16, :] = t[lo:lo + 16, :]
    pl.semaphore_wait(barrier, owners - 1 + 5)

    def plane_copy(tile, at, n, send, recv, move):
        here = pl.ds(2 * tile + at, n)
        return pltpu.make_async_remote_copy(
            src_ref=xt.at[here],
            dst_ref=xt.at[here],
            send_sem=send,
            recv_sem=recv,
            device_id=dev(dp, shift(move)),
            device_id_type=MESH,
        )

    def quarter_copy(tile, q, h, send, recv, move):
        return pltpu.make_async_remote_copy(
            src_ref=xt.at[2 * tile + q, h],
            dst_ref=xt.at[2 * tile + q, h],
            send_sem=send,
            recv_sem=recv,
            device_id=dev(dp, shift(move)),
            device_id_type=MESH,
        )

    def near_copy(v, tile):
        i = NEAR.index(v)
        return plane_copy(tile, 0, 2, ag_send.at[i], ag_recv.at[i], v)

    def relay_copies(v, tile):
        dy, dx = v
        i = NEAR.index(v)
        out = []
        if dx:
            q = 0 if dx > 0 else 1
            out.append(plane_copy(tile, q, 1, rl_send.at[0, i], rl_recv.at[0, i], (0, dx)))
        if dy:
            q = 0 if dy > 0 else 1
            out.append(plane_copy(tile, q, 1, rl_send.at[1, i], rl_recv.at[1, i], (dy, 0)))
        if dx and dy:
            q, h = 0 if dy > 0 else 1, 0 if dx > 0 else 1
            out.append(quarter_copy(tile, q, h, rl_send.at[2, i], rl_recv.at[2, i], v))
        return out

    def relayed_copies(u, tile):
        dy, dx = u
        out = []
        if dx == 2 and dy != 2:
            for d in (1, -1):
                out.append(relay_copies((dy, d), tile)[0])
        elif dy == 2 and dx != 2:
            for d in (1, -1):
                out.append(relay_copies((d, dx), tile)[1 if dx else 0])
        else:
            for d in (1, -1):
                for e in (1, -1):
                    out.append(relay_copies((d, e), tile)[2])
        return out

    def sib_copy(i, tile):
        return pltpu.make_async_remote_copy(
            src_ref=xt.at[pl.ds(2 * tile, 2), other],
            dst_ref=sib.at[pl.ds(2 * tile, 2)],
            send_sem=sib_send.at[i],
            recv_sem=sib_recv.at[i],
            device_id=dev(sibling, me),
            device_id_type=MESH,
        )

    def dx_copy(o):
        return pltpu.make_async_remote_copy(
            src_ref=dxs.at[o],
            dst_ref=dxr.at[o],
            send_sem=dx_send.at[o],
            recv_sem=dx_recv.at[o],
            device_id=dev(dp, peer_to(o)),
            device_id_type=MESH,
        )

    def pair_copy(way, step, piece):
        at = pl.ds(piece * group, group)
        return pltpu.make_async_remote_copy(
            src_ref=pair_send.at[way, step, at],
            dst_ref=pair_recv.at[way, step, at],
            send_sem=ps_send.at[way, step, piece],
            recv_sem=ps_recv.at[way, step, piece],
            device_id=along(way, 1),
            device_id_type=MESH,
        )

    def chain_copy(way, step, piece):
        at = pl.ds(piece * group, group)
        return pltpu.make_async_remote_copy(
            src_ref=chain_send.at[way, step, at],
            dst_ref=chain_recv.at[way, step, at],
            send_sem=cs_send.at[way, step, piece],
            recv_sem=cs_recv.at[way, step, piece],
            device_id=along(way, 2),
            device_id_type=MESH,
        )

    g_copy = pltpu.make_async_remote_copy(
        src_ref=gcat.at[0],
        dst_ref=gcat.at[1],
        send_sem=gsib_sem.at[0],
        recv_sem=gsib_sem.at[1],
        device_id=dev(sibling, me),
        device_id_type=MESH,
    )

    for v in NEAR:
        near_copy(v, me).start()

    sib_copy(0, me).start()
    g_load.wait()
    g_copy.start()

    n_cols = co_ref.shape[1]
    mine = (co_ref[...] == me).astype(jnp.int32)
    sub = lax.broadcasted_iota(jnp.int32, (n_cols, n_cols), 0)
    lane = lax.broadcasted_iota(jnp.int32, (n_cols, n_cols), 1)
    mine_col = jnp.sum(jnp.where(sub == lane, mine, 0), axis=1, keepdims=True)
    rank = jnp.sum(jnp.where(sub < lane, mine_col, 0), axis=0, keepdims=True)
    slot_id = lax.broadcasted_iota(jnp.int32, (16, n_cols), 0)
    chosen = jnp.where((rank == slot_id) & (slot_id < slots), mine, 0)
    live_col = jnp.sum(chosen, axis=1, keepdims=True)
    tl = lax.broadcasted_iota(jnp.int32, (16, 128), 1)
    table = jnp.where(tl < row_tiles, per_col, 0)
    for k in range(per_col):
        row_col = jnp.sum(chosen * trt_ref[k:k + 1, :], axis=1, keepdims=True)
        found = (live_col == 1) & (tl < row_tiles) & (tl == row_col)
        table = jnp.where(found, k, jnp.where(tl == row_tiles + k, row_col, table))
    table = jnp.where(tl == row_tiles + per_col, live_col, table)
    tbl[...] = table
    tbl_copy = pltpu.make_async_copy(tbl, tbl_s, tbl_sem)
    tbl_copy.start()

    for s in range(slots):
        w[s, per_col] = jnp.zeros((128, 128), BF16)
        gt[s * 128:(s + 1) * 128, :] = g_ref[:, s * 128:(s + 1) * 128].T

    tbl_copy.wait()
    w_copy.wait()

    def dx_terms(o):
        owner = peer_to(o)
        for q in range(2):
            r = 2 * owner + q
            lhs = jnp.concatenate([w[s, tbl_s[s, r]] for s in range(slots)], axis=1)
            dxs[o, q] = jnp.dot(lhs, gt[...], preferred_element_type=F32).astype(BF16)

    early = 1 + (owners - 1) * 2 // 5

    @pl.loop(1, early)
    def _(o):
        dx_terms(o)

    for i, v in enumerate(NEAR):
        tile = shift((-v[0], -v[1]))
        near_copy(v, tile).wait_recv()
        for copy in relay_copies(v, tile):
            copy.start()
        sib_copy(1 + i, tile).start()

    @pl.loop(early, owners)
    def _(o):
        dx_terms(o)

    for i, u in enumerate(FAR):
        tile = shift((-u[0], -u[1]))
        for copy in relayed_copies(u, tile):
            copy.wait_recv()
        sib_copy(1 + len(NEAR) + i, tile).start()

    sib_copy(0, me).wait_recv()
    for i, v in enumerate(NEAR + FAR):
        sib_copy(1 + i, shift((-v[0], -v[1]))).wait_recv()

    g_copy.wait_recv()

    def dw_terms(ks):
        @pl.loop(0, slots, unroll=4)
        def _(s):
            rows = [tbl_s[s, row_tiles + k] for k in ks]
            lhs = jnp.concatenate(
                [jnp.concatenate([xt[rk, core] for rk in rows], axis=0), jnp.concatenate([sib[rk] for rk in rows], axis=0)],
                axis=1,
            )
            lanes = pl.ds(pl.multiple_of(s * 128, 128), 128)
            rhs = jnp.concatenate([gcat[0, :, lanes], gcat[1, :, lanes]], axis=0)
            res = jnp.dot(lhs, rhs, preferred_element_type=F32)
            for j, k in enumerate(ks):
                for gi in range(4):
                    lo = j * 64 + gi * 16
                    part[4 * k + gi, s] = res[lo:lo + 16, :]

    first = ((z + half - 1) % nz) // 4
    dw_rounds = (per_col - 2) // 2

    def dw_round(step):
        dw_terms([(first + 2 * per_col - 1 - step) % per_col, (first + 2 + step) % per_col])

    def dest(way, links):
        return (z + links) % nz if way == 0 else (z + nz - links) % nz

    def send_pair(way, step, piece):
        at = pl.ds(piece * group, group)
        pair_send[way, step, at] = part[dest(way, half - 1 - 2 * step), at].astype(BF16)
        pair_copy(way, step, piece).start()

    def send_chain(way, step, piece, paired=True, chained=True):
        at = pl.ds(piece * group, group)
        total = part[dest(way, half - 2 * step), at]
        if paired:
            pair_copy(way, step - 1, piece).wait_recv()
            total = total + pair_recv[way, step - 1, at].astype(F32)
        if chained:
            chain_copy(way, step - 1, piece).wait_recv()
            total = total + chain_recv[way, step - 1, at].astype(F32)
        chain_send[way, step, at] = total.astype(BF16)
        chain_copy(way, step, piece).start()

    dw_terms([first, (first + 1) % per_col] if per_col > 1 else [first])
    for piece in range(PIECES):
        send_chain(0, 0, piece, paired=False, chained=False)
        for way in range(2):
            send_pair(way, 0, piece)

    @pl.loop(1, owners)
    def _(o):
        dx_copy(o).start()

    turn_steps = 4
    turn_tiles = row_tiles // turn_steps

    def unit(u):
        @pl.when(u < turn_steps)
        def _():
            for j in range(turn_tiles):
                r = u * turn_tiles + j
                t = jnp.concatenate([xt[r, h, gi * 16:(gi + 1) * 16, :] for gi in range(4) for h in range(2)], axis=0)
                xn[r] = t.T

        @pl.when((u >= turn_steps) & (u < turn_steps + slots))
        def _():
            s = u - turn_steps
            lhs = jnp.concatenate([xn[tbl_s[s, row_tiles + k]] for k in range(per_col)], axis=1)
            rhs = jnp.concatenate([w[s, k] for k in range(per_col)], axis=0)
            live = tbl_s[s, row_tiles + per_col].astype(F32)
            out = jnp.dot(lhs, rhs, preferred_element_type=F32) * live
            out_ref[:, pl.ds(pl.multiple_of(s * 128, 128), 128)] = out.astype(BF16)

    per_step = (turn_steps + slots) // steps

    def units(step):
        for u in range(per_step):
            unit(step * per_step + u)

    if dw_rounds > 0:
        dw_round(0)
    units(0)

    if steps > 1:
        for piece in range(PIECES):
            send_chain(0, 1, piece)
            send_chain(1, 1, piece, chained=False)
            for way in range(2):
                send_pair(way, 1, piece)
        if dw_rounds > 1:
            dw_round(1)
        units(1)

    @pl.loop(2, steps)
    def _(step):
        for piece in range(PIECES):
            for way in range(2):
                send_chain(way, step, piece)
            for way in range(2):
                send_pair(way, step, piece)

        @pl.when(step < dw_rounds)
        def _():
            dw_round(step)

        units(step)

    dx_terms(0)

    def dx_add(o, total):
        dx_copy(o).wait_recv()
        return total + dxr[o].astype(F32)

    dx = lax.fori_loop(1, owners, dx_add, dxs[0].astype(F32))
    for q in range(2):
        dx_ref[:, q * 128:(q + 1) * 128] = dx[q].T.astype(BF16)

    totals = []
    for piece in range(PIECES):
        at = pl.ds(piece * group, group)
        total = part[z, at]
        for way in range(2):
            pair_copy(way, steps - 1, piece).wait_recv()
            total = total + pair_recv[way, steps - 1, at].astype(F32)
            if way == 0 or steps > 1:
                chain_copy(way, steps - 1, piece).wait_recv()
                total = total + chain_recv[way, steps - 1, at].astype(F32)
        totals += [total[i] * (tbl_s[piece * group + i, row_tiles + per_col].astype(F32) * scale) for i in range(group)]
    total = jnp.stack(totals)
    for i in range(16):
        dw_ref[:, i * 128:(i + 1) * 128] = total[:, i, :]

    @pl.loop(1, owners)
    def _(o):
        dx_copy(o).wait_send()

    for v in NEAR:
        near_copy(v, me).wait_send()
        for copy in relay_copies(v, me):
            copy.wait_send()

    @pl.loop(0, owners)
    def _(i):
        sib_copy(i, me).wait_send()

    g_copy.wait_send()

    for way in range(2):
        for piece in range(PIECES):
            pair_copy(way, 0, piece).wait_send()
            if way == 0:
                chain_copy(way, 0, piece).wait_send()

    @pl.loop(1, steps)
    def _(step):
        for piece in range(PIECES):
            for way in range(2):
                chain_copy(way, step, piece).wait_send()
                pair_copy(way, step, piece).wait_send()


def finish(a_ref, b_ref, c_ref, x_ref, y_ref, z_ref, a, b, c, load_sem, store_sem):
    loads, stores = [], []
    for i, (src, held, dst) in enumerate(((a_ref, a, x_ref), (b_ref, b, y_ref), (c_ref, c, z_ref))):
        loads.append(pltpu.make_async_copy(src, held, load_sem.at[i]))
        stores.append(pltpu.make_async_copy(held, dst, store_sem.at[i]))
    for load in loads:
        load.start()
    for load, store in zip(loads, stores):
        load.wait()
        store.start()
    for store in stores:
        store.wait()


def local(ny, nx, n_dp, activations, weight_tiles, grad_out, tile_rows, col_owner):
    tokens, features = activations.shape
    slots, per_col = weight_tiles.shape[:2]
    owners = ny * nx
    nz = n_dp // 2
    steps = nz // 4
    row_tiles = 2 * owners
    scale = 1.0 / math.sqrt(tokens * n_dp)
    vmem = pl.BlockSpec(memory_space=pltpu.VMEM)
    hbm = pl.BlockSpec(memory_space=pltpu.HBM)
    dma = pltpu.SemaphoreType.DMA
    results = pl.pallas_call(
        functools.partial(kernel, (ny, nx, nz, slots, per_col, scale)),
        out_shape=(
            jax.ShapeDtypeStruct(grad_out.shape, BF16),
            jax.ShapeDtypeStruct(activations.shape, BF16),
            jax.ShapeDtypeStruct((slots, 2048), F32),
        ),
        in_specs=[hbm, hbm, hbm, vmem, vmem],
        out_specs=(vmem, vmem, vmem),
        scratch_shapes=[
            pltpu.VMEM(activations.shape, BF16),
            pltpu.VMEM((row_tiles, 2, 64, tokens), BF16),
            pltpu.VMEM((row_tiles, 64, tokens), BF16),
            pltpu.VMEM((row_tiles, tokens, 128), BF16),
            pltpu.VMEM((slots, per_col + 1, 128, 128), BF16),
            pltpu.VMEM((2, tokens, slots * 128), BF16),
            pltpu.VMEM((slots * 128, tokens), BF16),
            pltpu.VMEM((owners, 2, 128, tokens), BF16),
            pltpu.VMEM((owners, 2, 128, tokens), BF16),
            pltpu.VMEM((nz, slots, 16, 128), F32),
            pltpu.VMEM((2, steps, slots, 16, 128), BF16),
            pltpu.VMEM((2, steps, slots, 16, 128), BF16),
            pltpu.VMEM((2, steps, slots, 16, 128), BF16),
            pltpu.VMEM((2, steps, slots, 16, 128), BF16),
            pltpu.VMEM((16, 128), jnp.int32),
            pltpu.SMEM((16, 128), jnp.int32),
            dma((3,)),
            dma(()),
            dma((2,)),
            dma((8,)),
            dma((8,)),
            dma((3, 8)),
            dma((3, 8)),
            dma((owners,)),
            dma((owners,)),
            dma((owners,)),
            dma((owners,)),
            dma((2, steps, PIECES)),
            dma((2, steps, PIECES)),
            dma((2, steps, PIECES)),
            dma((2, steps, PIECES)),
        ],
        compiler_params=pltpu.CompilerParams(
            collective_id=0, has_side_effects=True, vmem_limit_bytes=60 * 1024 * 1024
        ),
    )(activations, weight_tiles, grad_out, tile_rows.T, col_owner.reshape(1, -1))
    return pl.pallas_call(
        finish,
        out_shape=tuple(jax.ShapeDtypeStruct(r.shape, r.dtype) for r in results),
        in_specs=[hbm] * 3,
        out_specs=(hbm,) * 3,
        scratch_shapes=[pltpu.VMEM(r.shape, r.dtype) for r in results] + [dma((3,)), dma((3,))],
    )(*results)


def solution(mesh):
    owners, n_dp = mesh.shape["owner"], mesh.shape["dp"]
    nx = math.isqrt(owners)
    in_specs = (P("dp", "owner"), P("owner", None, None, None), P("dp", "owner"), P(), P())
    out_specs = (P("dp", "owner"), P("dp", "owner"), P("owner", "dp"))
    return jax.shard_map(
        functools.partial(local, owners // nx, nx, n_dp),
        mesh=mesh,
        in_specs=in_specs,
        out_specs=out_specs,
        check_vma=False,
    )
```

```python
import functools
import math

import jax
import jax.numpy as jnp
from jax import lax
from jax.experimental import pallas as pl
from jax.experimental.pallas import tpu as pltpu
from jax.sharding import PartitionSpec as P

MESH = pl.DeviceIdType.MESH
F32 = jnp.float32
BF16 = jnp.bfloat16
PIECES = 3
NEAR = [(1, 1), (1, -1), (-1, 1), (-1, -1), (0, 1), (0, -1), (1, 0), (-1, 0)]
FAR = [(0, 2), (1, 2), (-1, 2), (2, 0), (2, 1), (2, -1), (2, 2)]


def kernel(
    dims,
    x_hbm, w_hbm, g_hbm, trt_ref, co_ref,
    out_ref, dx_ref, dw_ref,
    x_ref, xt, sib, xn, w, gcat, gt, dxs, dxr, part, pair_send, pair_recv, chain_send, chain_recv, tbl, tbl_s,
    in_sem, tbl_sem, gsib_sem, ag_send, ag_recv, rl_send, rl_recv, sib_send, sib_recv, dx_send, dx_recv,
    ps_send, ps_recv, cs_send, cs_recv,
):
    ny, nx, nz, slots, per_col, scale = dims
    owners = ny * nx
    half = nz // 2
    steps = half // 2
    group = slots // PIECES
    row_tiles = 2 * owners
    dp = lax.axis_index("dp")
    me = lax.axis_index("owner")
    z, core = dp // 2, dp % 2
    other = 1 - core
    y, x = me // nx, me % nx

    def dev(d, o):
        return {"dp": d, "owner": o}

    def peer_to(o):
        return ((y + o // nx) % ny) * nx + (x + o % nx) % nx

    def shift(v):
        return ((y + ny + v[0]) % ny) * nx + (x + nx + v[1]) % nx

    def along(way, links):
        return dev(((z + links) % nz if way == 0 else (z + nz - links) % nz) * 2 + core, me)

    sibling = z * 2 + other

    x_copy = pltpu.make_async_copy(x_hbm, x_ref, in_sem.at[0])
    g_load = pltpu.make_async_copy(g_hbm, gcat.at[0], in_sem.at[1])
    w_copy = pltpu.make_async_copy(w_hbm, w.at[:, pl.ds(0, per_col)], in_sem.at[2])
    x_copy.start()
    g_load.start()
    w_copy.start()
    g_ref = gcat.at[0]

    barrier = pltpu.get_barrier_semaphore()
    for v in NEAR:
        pl.semaphore_signal(barrier, inc=1, device_id=dev(dp, shift(v)), device_id_type=MESH)
    for d in (along(0, 1), along(1, 1), along(0, 2), along(1, 2), dev(sibling, me)):
        pl.semaphore_signal(barrier, inc=1, device_id=d, device_id_type=MESH)

    x_copy.wait()
    for q in range(2):
        t = x_ref[:, q * 128:(q + 1) * 128].T
        for gi in range(4):
            for h in range(2):
                lo = gi * 32 + h * 16
                xt[2 * me + q, h, gi * 16:(gi + 1) * 16, :] = t[lo:lo + 16, :]
    pl.semaphore_wait(barrier, len(NEAR) + 5)

    def plane_copy(tile, at, n, send, recv, move):
        here = pl.ds(2 * tile + at, n)
        return pltpu.make_async_remote_copy(
            src_ref=xt.at[here],
            dst_ref=xt.at[here],
            send_sem=send,
            recv_sem=recv,
            device_id=dev(dp, shift(move)),
            device_id_type=MESH,
        )

    def quarter_copy(tile, q, h, send, recv, move):
        return pltpu.make_async_remote_copy(
            src_ref=xt.at[2 * tile + q, h],
            dst_ref=xt.at[2 * tile + q, h],
            send_sem=send,
            recv_sem=recv,
            device_id=dev(dp, shift(move)),
            device_id_type=MESH,
        )

    def near_copy(v, tile):
        i = NEAR.index(v)
        return plane_copy(tile, 0, 2, ag_send.at[i], ag_recv.at[i], v)

    def relay_copies(v, tile):
        dy, dx = v
        i = NEAR.index(v)
        out = []
        if dx:
            q = 0 if dx > 0 else 1
            out.append(plane_copy(tile, q, 1, rl_send.at[0, i], rl_recv.at[0, i], (0, dx)))
        if dy:
            q = 0 if dy > 0 else 1
            out.append(plane_copy(tile, q, 1, rl_send.at[1, i], rl_recv.at[1, i], (dy, 0)))
        if dx and dy:
            q, h = 0 if dy > 0 else 1, 0 if dx > 0 else 1
            out.append(quarter_copy(tile, q, h, rl_send.at[2, i], rl_recv.at[2, i], v))
        return out

    def relayed_copies(u, tile):
        dy, dx = u
        out = []
        if dx == 2 and dy != 2:
            for d in (1, -1):
                out.append(relay_copies((dy, d), tile)[0])
        elif dy == 2 and dx != 2:
            for d in (1, -1):
                out.append(relay_copies((d, dx), tile)[1 if dx else 0])
        else:
            for d in (1, -1):
                for e in (1, -1):
                    out.append(relay_copies((d, e), tile)[2])
        return out

    def sib_copy(i, tile):
        return pltpu.make_async_remote_copy(
            src_ref=xt.at[pl.ds(2 * tile, 2), other],
            dst_ref=sib.at[pl.ds(2 * tile, 2)],
            send_sem=sib_send.at[i],
            recv_sem=sib_recv.at[i],
            device_id=dev(sibling, me),
            device_id_type=MESH,
        )

    def dx_copy(o):
        return pltpu.make_async_remote_copy(
            src_ref=dxs.at[o],
            dst_ref=dxr.at[o],
            send_sem=dx_send.at[o],
            recv_sem=dx_recv.at[o],
            device_id=dev(dp, peer_to(o)),
            device_id_type=MESH,
        )

    def pair_copy(way, step, piece):
        at = pl.ds(piece * group, group)
        return pltpu.make_async_remote_copy(
            src_ref=pair_send.at[way, step, at],
            dst_ref=pair_recv.at[way, step, at],
            send_sem=ps_send.at[way, step, piece],
            recv_sem=ps_recv.at[way, step, piece],
            device_id=along(way, 1),
            device_id_type=MESH,
        )

    def chain_copy(way, step, piece):
        at = pl.ds(piece * group, group)
        return pltpu.make_async_remote_copy(
            src_ref=chain_send.at[way, step, at],
            dst_ref=chain_recv.at[way, step, at],
            send_sem=cs_send.at[way, step, piece],
            recv_sem=cs_recv.at[way, step, piece],
            device_id=along(way, 2),
            device_id_type=MESH,
        )

    g_copy = pltpu.make_async_remote_copy(
        src_ref=gcat.at[0],
        dst_ref=gcat.at[1],
        send_sem=gsib_sem.at[0],
        recv_sem=gsib_sem.at[1],
        device_id=dev(sibling, me),
        device_id_type=MESH,
    )

    for v in NEAR:
        near_copy(v, me).start()

    sib_copy(0, me).start()
    g_load.wait()
    g_copy.start()

    n_cols = co_ref.shape[1]
    mine = (co_ref[...] == me).astype(jnp.int32)
    sub = lax.broadcasted_iota(jnp.int32, (n_cols, n_cols), 0)
    lane = lax.broadcasted_iota(jnp.int32, (n_cols, n_cols), 1)
    mine_col = jnp.sum(jnp.where(sub == lane, mine, 0), axis=1, keepdims=True)
    rank = jnp.sum(jnp.where(sub < lane, mine_col, 0), axis=0, keepdims=True)
    slot_id = lax.broadcasted_iota(jnp.int32, (16, n_cols), 0)
    chosen = jnp.where((rank == slot_id) & (slot_id < slots), mine, 0)
    live_col = jnp.sum(chosen, axis=1, keepdims=True)
    tl = lax.broadcasted_iota(jnp.int32, (16, 128), 1)
    table = jnp.where(tl < row_tiles, per_col, 0)
    for k in range(per_col):
        row_col = jnp.sum(chosen * trt_ref[k:k + 1, :], axis=1, keepdims=True)
        found = (live_col == 1) & (tl < row_tiles) & (tl == row_col)
        table = jnp.where(found, k, jnp.where(tl == row_tiles + k, row_col, table))
    table = jnp.where(tl == row_tiles + per_col, live_col, table)
    tbl[...] = table
    tbl_copy = pltpu.make_async_copy(tbl, tbl_s, tbl_sem)
    tbl_copy.start()

    for s in range(slots):
        w[s, per_col] = jnp.zeros((128, 128), BF16)
        gt[s * 128:(s + 1) * 128, :] = g_ref[:, s * 128:(s + 1) * 128].T

    tbl_copy.wait()
    w_copy.wait()

    def dx_terms(o):
        owner = peer_to(o)
        for q in range(2):
            r = 2 * owner + q
            lhs = jnp.concatenate([w[s, tbl_s[s, r]] for s in range(slots)], axis=1)
            dxs[o, q] = jnp.dot(lhs, gt[...], preferred_element_type=F32).astype(BF16)

    early = 1 + (owners - 1) * 2 // 5

    @pl.loop(1, early)
    def _(o):
        dx_terms(o)

    for i, v in enumerate(NEAR):
        tile = shift((-v[0], -v[1]))
        near_copy(v, tile).wait_recv()
        for copy in relay_copies(v, tile):
            copy.start()
        sib_copy(1 + i, tile).start()

    @pl.loop(early, owners)
    def _(o):
        dx_terms(o)

    for i, u in enumerate(FAR):
        tile = shift((-u[0], -u[1]))
        for copy in relayed_copies(u, tile):
            copy.wait_recv()
        sib_copy(1 + len(NEAR) + i, tile).start()

    sib_copy(0, me).wait_recv()
    for i, v in enumerate(NEAR + FAR):
        sib_copy(1 + i, shift((-v[0], -v[1]))).wait_recv()

    g_copy.wait_recv()

    def dw_terms(ks):
        @pl.loop(0, slots, unroll=4)
        def _(s):
            rows = [tbl_s[s, row_tiles + k] for k in ks]
            lhs = jnp.concatenate(
                [jnp.concatenate([xt[rk, core] for rk in rows], axis=0), jnp.concatenate([sib[rk] for rk in rows], axis=0)],
                axis=1,
            )
            lanes = pl.ds(pl.multiple_of(s * 128, 128), 128)
            rhs = jnp.concatenate([gcat[0, :, lanes], gcat[1, :, lanes]], axis=0)
            res = jnp.dot(lhs, rhs, preferred_element_type=F32)
            for j, k in enumerate(ks):
                for gi in range(4):
                    lo = j * 64 + gi * 16
                    part[4 * k + gi, s] = res[lo:lo + 16, :]

    first = ((z + half - 1) % nz) // 4
    dw_rounds = (per_col - 2) // 2

    def dw_round(step):
        dw_terms([(first + 2 * per_col - 1 - step) % per_col, (first + 2 + step) % per_col])

    def dest(way, links):
        return (z + links) % nz if way == 0 else (z + nz - links) % nz

    def send_pair(way, step, piece):
        at = pl.ds(piece * group, group)
        pair_send[way, step, at] = part[dest(way, half - 1 - 2 * step), at].astype(BF16)
        pair_copy(way, step, piece).start()

    def send_chain(way, step, piece, paired=True, chained=True):
        at = pl.ds(piece * group, group)
        total = part[dest(way, half - 2 * step), at]
        if paired:
            pair_copy(way, step - 1, piece).wait_recv()
            total = total + pair_recv[way, step - 1, at].astype(F32)
        if chained:
            chain_copy(way, step - 1, piece).wait_recv()
            total = total + chain_recv[way, step - 1, at].astype(F32)
        chain_send[way, step, at] = total.astype(BF16)
        chain_copy(way, step, piece).start()

    dw_terms([first, (first + 1) % per_col] if per_col > 1 else [first])
    for piece in range(PIECES):
        send_chain(0, 0, piece, paired=False, chained=False)
        for way in range(2):
            send_pair(way, 0, piece)

    @pl.loop(1, owners)
    def _(o):
        dx_copy(o).start()

    turn_steps = 4
    turn_tiles = row_tiles // turn_steps

    def unit(u):
        @pl.when(u < turn_steps)
        def _():
            for j in range(turn_tiles):
                r = u * turn_tiles + j
                t = jnp.concatenate([xt[r, h, gi * 16:(gi + 1) * 16, :] for gi in range(4) for h in range(2)], axis=0)
                xn[r] = t.T

        @pl.when((u >= turn_steps) & (u < turn_steps + slots))
        def _():
            s = u - turn_steps
            lhs = jnp.concatenate([xn[tbl_s[s, row_tiles + k]] for k in range(per_col)], axis=1)
            rhs = jnp.concatenate([w[s, k] for k in range(per_col)], axis=0)
            live = tbl_s[s, row_tiles + per_col].astype(F32)
            out = jnp.dot(lhs, rhs, preferred_element_type=F32) * live
            out_ref[:, pl.ds(pl.multiple_of(s * 128, 128), 128)] = out.astype(BF16)

    per_step = (turn_steps + slots) // steps

    def units(step):
        for u in range(per_step):
            unit(step * per_step + u)

    if dw_rounds > 0:
        dw_round(0)
    units(0)

    if steps > 1:
        for piece in range(PIECES):
            send_chain(0, 1, piece)
            send_chain(1, 1, piece, chained=False)
            for way in range(2):
                send_pair(way, 1, piece)
        if dw_rounds > 1:
            dw_round(1)
        units(1)

    @pl.loop(2, steps)
    def _(step):
        for piece in range(PIECES):
            for way in range(2):
                send_chain(way, step, piece)
            for way in range(2):
                send_pair(way, step, piece)

        @pl.when(step < dw_rounds)
        def _():
            dw_round(step)

        units(step)

    dx_terms(0)

    def dx_add(o, total):
        dx_copy(o).wait_recv()
        return total + dxr[o].astype(F32)

    dx = lax.fori_loop(1, owners, dx_add, dxs[0].astype(F32))
    for q in range(2):
        dx_ref[:, q * 128:(q + 1) * 128] = dx[q].T.astype(BF16)

    totals = []
    for piece in range(PIECES):
        at = pl.ds(piece * group, group)
        total = part[z, at]
        for way in range(2):
            pair_copy(way, steps - 1, piece).wait_recv()
            total = total + pair_recv[way, steps - 1, at].astype(F32)
            if way == 0 or steps > 1:
                chain_copy(way, steps - 1, piece).wait_recv()
                total = total + chain_recv[way, steps - 1, at].astype(F32)
        totals += [total[i] * (tbl_s[piece * group + i, row_tiles + per_col].astype(F32) * scale) for i in range(group)]
    total = jnp.stack(totals)
    for i in range(16):
        dw_ref[:, i * 128:(i + 1) * 128] = total[:, i, :]

    @pl.loop(1, owners)
    def _(o):
        dx_copy(o).wait_send()

    for v in NEAR:
        near_copy(v, me).wait_send()
        for copy in relay_copies(v, me):
            copy.wait_send()

    @pl.loop(0, owners)
    def _(i):
        sib_copy(i, me).wait_send()

    g_copy.wait_send()

    for way in range(2):
        for piece in range(PIECES):
            pair_copy(way, 0, piece).wait_send()
            if way == 0:
                chain_copy(way, 0, piece).wait_send()

    @pl.loop(1, steps)
    def _(step):
        for piece in range(PIECES):
            for way in range(2):
                chain_copy(way, step, piece).wait_send()
                pair_copy(way, step, piece).wait_send()


def finish(a_ref, b_ref, c_ref, x_ref, y_ref, z_ref, a, b, c, load_sem, store_sem):
    loads, stores = [], []
    for i, (src, held, dst) in enumerate(((a_ref, a, x_ref), (b_ref, b, y_ref), (c_ref, c, z_ref))):
        loads.append(pltpu.make_async_copy(src, held, load_sem.at[i]))
        stores.append(pltpu.make_async_copy(held, dst, store_sem.at[i]))
    for load in loads:
        load.start()
    for load, store in zip(loads, stores):
        load.wait()
        store.start()
    for store in stores:
        store.wait()


def local(ny, nx, n_dp, activations, weight_tiles, grad_out, tile_rows, col_owner):
    tokens, features = activations.shape
    slots, per_col = weight_tiles.shape[:2]
    owners = ny * nx
    nz = n_dp // 2
    steps = nz // 4
    row_tiles = 2 * owners
    scale = 1.0 / math.sqrt(tokens * n_dp)
    vmem = pl.BlockSpec(memory_space=pltpu.VMEM)
    hbm = pl.BlockSpec(memory_space=pltpu.HBM)
    dma = pltpu.SemaphoreType.DMA
    results = pl.pallas_call(
        functools.partial(kernel, (ny, nx, nz, slots, per_col, scale)),
        out_shape=(
            jax.ShapeDtypeStruct(grad_out.shape, BF16),
            jax.ShapeDtypeStruct(activations.shape, BF16),
            jax.ShapeDtypeStruct((slots, 2048), F32),
        ),
        in_specs=[hbm, hbm, hbm, vmem, vmem],
        out_specs=(vmem, vmem, vmem),
        scratch_shapes=[
            pltpu.VMEM(activations.shape, BF16),
            pltpu.VMEM((row_tiles, 2, 64, tokens), BF16),
            pltpu.VMEM((row_tiles, 64, tokens), BF16),
            pltpu.VMEM((row_tiles, tokens, 128), BF16),
            pltpu.VMEM((slots, per_col + 1, 128, 128), BF16),
            pltpu.VMEM((2, tokens, slots * 128), BF16),
            pltpu.VMEM((slots * 128, tokens), BF16),
            pltpu.VMEM((owners, 2, 128, tokens), BF16),
            pltpu.VMEM((owners, 2, 128, tokens), BF16),
            pltpu.VMEM((nz, slots, 16, 128), F32),
            pltpu.VMEM((2, steps, slots, 16, 128), BF16),
            pltpu.VMEM((2, steps, slots, 16, 128), BF16),
            pltpu.VMEM((2, steps, slots, 16, 128), BF16),
            pltpu.VMEM((2, steps, slots, 16, 128), BF16),
            pltpu.VMEM((16, 128), jnp.int32),
            pltpu.SMEM((16, 128), jnp.int32),
            dma((3,)),
            dma(()),
            dma((2,)),
            dma((8,)),
            dma((8,)),
            dma((3, 8)),
            dma((3, 8)),
            dma((owners,)),
            dma((owners,)),
            dma((owners,)),
            dma((owners,)),
            dma((2, steps, PIECES)),
            dma((2, steps, PIECES)),
            dma((2, steps, PIECES)),
            dma((2, steps, PIECES)),
        ],
        compiler_params=pltpu.CompilerParams(
            collective_id=0, has_side_effects=True, vmem_limit_bytes=60 * 1024 * 1024
        ),
    )(activations, weight_tiles, grad_out, tile_rows.T, col_owner.reshape(1, -1))
    return pl.pallas_call(
        finish,
        out_shape=tuple(jax.ShapeDtypeStruct(r.shape, r.dtype) for r in results),
        in_specs=[hbm] * 3,
        out_specs=(hbm,) * 3,
        scratch_shapes=[pltpu.VMEM(r.shape, r.dtype) for r in results] + [dma((3,)), dma((3,))],
    )(*results)


def solution(mesh):
    owners, n_dp = mesh.shape["owner"], mesh.shape["dp"]
    nx = math.isqrt(owners)
    in_specs = (P("dp", "owner"), P("owner", None, None, None), P("dp", "owner"), P(), P())
    out_specs = (P("dp", "owner"), P("dp", "owner"), P("owner", "dp"))
    return jax.shard_map(
        functools.partial(local, owners // nx, nx, n_dp),
        mesh=mesh,
        in_specs=in_specs,
        out_specs=out_specs,
        check_vma=False,
    )
```
